128 devices in a mesh: grp: 4 (over z_lo, core), blk: 32 (over x, y, z_hi).
Axes of the slice: x: 4, y: 4, z: 4 (z_hi: 2, z_lo: 2; z = z_hi * 2 + z_lo), core: 2. Of those that a mesh axis runs over, the one named last changes fastest.
Arguments:
- embeddings: bfloat16 [98304, 512], P(('grp', 'blk')), may hold values from -6 to 6
- cluster_ids: int32 [98304], P(('grp', 'blk')), may hold values from 0 to 11, as said below
Outputs:
- best: float32 [98304], P(('grp', 'blk'))
- cluster_mean: float32 [12], replicated
The draws below stay inside these ranges and needn't reach their ends.
Inputs may be any that keep to these rules, and one draw needn't show every extreme that they name: `cluster_ids`: items of one cluster are contiguous and lie within one block of 24576 items (group g holds clusters 3 * g to 3 * g + 2, each non-empty with 3072 items or more); ids never fall along the items.
All inputs are finite; a program needn't handle non-finite values.
Results may differ from the reference program's by a relative error of at most 0.0012.
Values may be sent and summed in bfloat16 or wider, within the bound.
A program may use at most 64 MiB of HBM per device.

```python
import jax
import jax.numpy as jnp
from jax import lax

D = 512
ROWS_DEV = 768
CL_GRP = 3
GROUP_ROWS = 24576
CLUSTERS = 12
ITEMS = 98304
N_GRP = 4


def draw_cluster_ids(key, part):
    key = jax.random.fold_in(key, 7)
    first, second = jax.random.split(key)
    groups = ITEMS // GROUP_ROWS
    cut_low = jax.random.randint(first, (groups,), GROUP_ROWS // 8, GROUP_ROWS * 3 // 8)
    cut_high = jax.random.randint(second, (groups,), GROUP_ROWS // 2, GROUP_ROWS * 7 // 8)
    positions = jnp.arange(GROUP_ROWS, dtype=jnp.int32)
    local = (positions[None, :] >= cut_low[:, None]).astype(jnp.int32) + (positions[None, :] >= cut_high[:, None]).astype(jnp.int32)
    ids = jnp.arange(groups, dtype=jnp.int32)[:, None] * CL_GRP + local
    return ids.reshape(ITEMS).astype(jnp.int32)


def shard_levels(stream_key, shape, cuts, low, largest):
    loudness = 1.0
    for position, shards_of in cuts:
        heights = jax.random.uniform(jax.random.fold_in(jax.random.fold_in(stream_key, 6), position), (shards_of,), jnp.float32, low / len(cuts), largest / len(cuts))
        loudness = loudness * jnp.repeat(jnp.exp(heights), shape[position] // shards_of).reshape((-1,) + (1,) * (len(shape) - 1 - position))
    return loudness


def centred(rng, shape, spread, limit, cuts=(), kind=jnp.bfloat16):
    entries = spread * jax.random.normal(rng, shape, jnp.float32)
    if cuts:
        entries = entries * shard_levels(rng, shape, cuts, -0.22, 0.18)
    return jnp.clip(entries, -limit, limit).astype(kind)


def setup_inputs(seed: int = 0) -> dict:
    arg_keys = jax.random.split(jax.random.key(seed), 3)
    return {
        "embeddings": centred(arg_keys[0], (ITEMS, D), 1.0, 6.0, ((0, 128),)),
        "cluster_ids": draw_cluster_ids(jax.random.fold_in(arg_keys[2], 71), 0),
    }


def reference(embeddings, cluster_ids):
    wide = embeddings.astype(jnp.float32)
    norms = lax.optimization_barrier(jnp.sum(wide * wide, axis=1))
    unit = (wide * lax.rsqrt(norms + 1e-06)[:, None]).astype(jnp.bfloat16)
    unit_wide = unit.astype(jnp.float32)
    groups = unit_wide.reshape(N_GRP, GROUP_ROWS, D)
    group_ids = cluster_ids.reshape(N_GRP, GROUP_ROWS)
    blocks = GROUP_ROWS // ROWS_DEV
    columns = jnp.arange(GROUP_ROWS, dtype=jnp.int32)

    def one_group(item):
        members, member_ids = item

        def one_block(index):
            start = (index * ROWS_DEV).astype(jnp.int32)
            rows = lax.dynamic_slice_in_dim(members, start, ROWS_DEV, 0)
            row_ids = lax.dynamic_slice_in_dim(member_ids, start, ROWS_DEV, 0)
            scores = jnp.dot(rows, members.T, precision=lax.Precision.HIGHEST, preferred_element_type=jnp.float32)
            positions = start + jnp.arange(ROWS_DEV, dtype=jnp.int32)
            same = (row_ids[:, None] == member_ids[None, :]) & (positions[:, None] != columns[None, :])
            return lax.optimization_barrier(jnp.max(jnp.where(same, scores, jnp.float32(-4.0)), axis=1))
        return lax.map(one_block, jnp.arange(blocks, dtype=jnp.int32)).reshape(GROUP_ROWS)
    best = lax.map(one_group, (groups, group_ids)).reshape(ITEMS)
    onehot = (cluster_ids[:, None] == jnp.arange(CLUSTERS, dtype=jnp.int32)[None, :]).astype(jnp.float32)
    sums = jnp.dot(best, onehot, precision=lax.Precision.HIGHEST, preferred_element_type=jnp.float32)
    counts = lax.optimization_barrier(jnp.sum(onehot, axis=0))
    return (best, sums / counts)
```

```python
import functools

import jax
import jax.numpy as jnp
from jax import lax
from jax.experimental import pallas as pl
from jax.experimental.pallas import tpu as pltpu
from jax.sharding import PartitionSpec as P

MESH = pl.DeviceIdType.MESH
CL_GRP = 3
FLOOR = -4.0
PIECE = 128
TILE = 256

OWN, B, C, F, G, A, E, RELAY = range(8)
HELD = {B: (1, 0, 0), C: (1, 1, 0), F: (0, 3, 1), G: (3, 0, 1), A: (3, 0, 0), E: (1, 2, 0)}
LINKS = {
    A: (OWN, (1, 0, 0)),
    B: (OWN, (3, 0, 0)),
    C: (B, (0, 3, 0)),
    E: (C, (0, 3, 0)),
    RELAY: (OWN, (0, 0, 1)),
    F: (RELAY, (0, 1, 0)),
    G: (RELAY, (1, 0, 0)),
}
WHOLE = ((B, OWN), (C, OWN), (C, B), (A, C), (F, OWN), (F, B), (F, C), (G, OWN), (G, B), (G, C), (G, F), (E, OWN))
HALVED = ((A, B), (F, A), (G, A), (E, B), (E, F), (E, G), (E, A))
PASS, SEND, TILE_OF = range(3)
ORDER = (
    (TILE_OF, OWN, 0), (TILE_OF, OWN, 1), (TILE_OF, OWN, 2),
    (PASS, B, 0), (PASS, RELAY, 0), (PASS, B, 1), (PASS, B, 2), (TILE_OF, B, 0), (PASS, RELAY, 1), (PASS, C, 0),
    (PASS, B, 3), (TILE_OF, B, 1), (PASS, C, 1), (PASS, RELAY, 2), (TILE_OF, A, 0), (PASS, B, 4), (PASS, C, 2),
    (TILE_OF, F, 0), (TILE_OF, G, 0), (PASS, RELAY, 3), (TILE_OF, C, 0), (PASS, B, 5), (PASS, C, 3), (TILE_OF, B, 2),
    (PASS, RELAY, 4), (SEND, A, 3), (PASS, C, 4), (TILE_OF, C, 1), (TILE_OF, F, 1), (TILE_OF, G, 1), (PASS, RELAY, 5),
    (SEND, A, 4), (SEND, A, 5), (PASS, C, 5), (TILE_OF, E, 0), (TILE_OF, C, 2), (TILE_OF, E, 1), (TILE_OF, F, 2),
    (TILE_OF, G, 2), (TILE_OF, A, 1), (TILE_OF, A, 2), (TILE_OF, E, 2),
)


def kernel(x_hbm, ids_hbm, best_ref, mean_ref, x_ref, ids_ref, held, row_max, col_max, row_ids, col_ids, counts, back, got,
           sums, total, x_sem, send_sem, recv_sem, ids_send, ids_recv, back_send, back_recv, sum_send, sum_recv, tot_send,
           tot_recv):
    rows, width = x_ref.shape
    pieces, tiles = rows // PIECE, rows // TILE
    grp, blk = lax.axis_index("grp"), lax.axis_index("blk")
    x, y, z = blk // 8, (blk // 2) % 4, blk % 2
    swap = (z + grp) % 2

    def load(q):
        window = pl.ds(q * PIECE, PIECE)
        return pltpu.make_async_copy(x_hbm.at[window], x_ref.at[window], x_sem.at[q])

    load_ids = pltpu.make_async_copy(ids_hbm, ids_ref, x_sem.at[pieces])
    load_ids.start()
    for q in range(pieces):
        load(q).start()

    def place(nx, ny, nz):
        return (lax.rem(nx + 8, 4) * 4 + lax.rem(ny + 8, 4)) * 2 + lax.rem(nz, 2)

    def times(step):
        dx, dy, dz = step
        return (grp, place(x + dx * (1 - swap) + dy * swap, y + dy * (1 - swap) + dx * swap, z + dz))

    plane = [(dx, dy) for dx in range(4) for dy in range(4) if dx or dy]
    across = [(dz, dg) for dz in range(2) for dg in range(4) if dz or dg]

    def in_plane(dx, dy):
        return (grp, place(x + dx, y + dy, z))

    def over(dz, dg):
        return (lax.rem(grp + dg, 4), place(x, y, z + dz))

    barrier = pltpu.get_barrier_semaphore()
    greeted = [in_plane(*p) for p in ((0, 1), (0, 3), (1, 0), (3, 0))] + [over(*a) for a in across]
    for device in greeted:
        pl.semaphore_signal(barrier, inc=1, device_id=device, device_id_type=MESH)

    def copy(slot, q):
        source, step = LINKS[slot]
        window = pl.ds(q * PIECE, PIECE)
        return pltpu.make_async_remote_copy(
            src_ref=held.at[source, window], dst_ref=held.at[slot, window], send_sem=send_sem.at[slot - 1, q],
            recv_sem=recv_sem.at[slot - 1, q], device_id=times(step), device_id_type=MESH)

    def ids_copy(slot):
        source, step = LINKS[slot]
        return pltpu.make_async_remote_copy(
            src_ref=counts.at[source], dst_ref=counts.at[slot], send_sem=ids_send.at[slot - 1],
            recv_sem=ids_recv.at[slot - 1], device_id=times(step), device_id_type=MESH)

    def back_copy(slot):
        return pltpu.make_async_remote_copy(
            src_ref=back.at[slot], dst_ref=got.at[slot], send_sem=back_send.at[slot - 1],
            recv_sem=back_recv.at[slot - 1], device_id=times(HELD[slot]), device_id_type=MESH)

    def normalise(q):
        load(q).wait()
        window = pl.ds(q * PIECE, PIECE)
        wide = x_ref[window, :].astype(jnp.float32)
        norms = jnp.sum(wide * wide, axis=1, keepdims=True)
        held[OWN, window, :] = (wide * lax.rsqrt(norms + 1e-06)).astype(jnp.bfloat16)

    def fill_ids(slot):
        low, high = counts[slot, 0:1, :], counts[slot, 1:2, :]
        at = lax.broadcasted_iota(jnp.int32, (rows, 128), 0).astype(jnp.float32)
        row_ids[slot] = (at >= low).astype(jnp.float32) + (at >= high).astype(jnp.float32)
        for j in range(rows // 128):
            at = (lax.broadcasted_iota(jnp.int32, (8, 128), 1) + 128 * j).astype(jnp.float32)
            col_ids[slot, :, pl.ds(128 * j, 128)] = (at >= low).astype(jnp.float32) + (at >= high).astype(jnp.float32)

    def product(j, first, n, s, q, diagonal=False):
        window = pl.ds(q * TILE, TILE)
        scores = lax.dot_general(held[j, pl.ds(first, n), :], held[s, window, :], (((1,), (1,)), ((), ())),
                                 preferred_element_type=jnp.float32)
        ids = row_ids[j, pl.ds(first, n), :]
        same = jnp.concatenate([ids] * (TILE // 128), axis=1) == col_ids[s, 0:1, window]
        if diagonal:
            same = same & (lax.broadcasted_iota(jnp.int32, (n, TILE), 0) != lax.broadcasted_iota(jnp.int32, (n, TILE), 1))
        masked = jnp.where(same, scores, jnp.float32(FLOOR))
        across_tile = functools.reduce(jnp.maximum, [masked[:, 128 * t:128 * t + 128] for t in range(TILE // 128)])
        row_max[j, pl.ds(first, n), :] = jnp.maximum(row_max[j, pl.ds(first, n), :], across_tile)
        if not diagonal:
            down = jnp.max(masked.reshape(n // 8, 8, TILE), axis=0)
            col_max[s, :, window] = jnp.maximum(col_max[s, :, window], down)

    waited, ready, tiles_in = set(), set(), set()

    def wait(slot, q):
        if (slot, q) not in waited:
            waited.add((slot, q))
            copy(slot, q).wait_recv()

    def wait_ids(slot):
        if slot not in ready:
            ready.add(slot)
            ids_copy(slot).wait_recv()
            if slot != RELAY:
                fill_ids(slot)

    def wanted(s, q, j, r):
        if (s, j) in WHOLE or (j, s) in WHOLE:
            return True
        return ((s, j) in HALVED and r >= q) or ((j, s) in HALVED and q >= r)

    def multiply(s, q):
        tiles_in.add((s, q))
        if s == OWN:
            product(OWN, q * TILE, TILE, OWN, q, diagonal=True)
            if q + 1 < tiles:
                product(OWN, (q + 1) * TILE, rows - (q + 1) * TILE, OWN, q)
            return
        for p in range(q * TILE // PIECE, (q + 1) * TILE // PIECE):
            wait(s, p)
        wait_ids(s)
        for j in (OWN, *HELD):
            if j == s:
                continue
            r = 0
            while r < tiles:
                end = r
                while end < tiles and (j, end) in tiles_in and wanted(s, q, j, end):
                    end += 1
                if end > r:
                    product(j, r * TILE, (end - r) * TILE, s, q)
                r = end + 1

    def pass_on(slot, q):
        wait(slot, q)
        onward = [to for to, (source, _) in LINKS.items() if source == slot]
        for to in onward:
            copy(to, q).start()
        if q == 0:
            wait_ids(slot)
            for to in onward:
                ids_copy(to).start()

    load_ids.wait()
    ids = ids_ref[...].reshape(1, rows)
    base = grp * CL_GRP
    low = jnp.sum((ids <= base).astype(jnp.float32), axis=1, keepdims=True)
    high = jnp.sum((ids <= base + 1).astype(jnp.float32), axis=1, keepdims=True)
    counts[OWN] = jnp.where(lax.broadcasted_iota(jnp.int32, (8, 128), 0) == 0, low, high)

    normalise(0)
    pl.semaphore_wait(barrier, len(greeted))
    early = [q for q in range(pieces) if (SEND, A, q) not in ORDER]
    for q in range(pieces):
        if q:
            normalise(q)
        for slot in (B, RELAY, A):
            if slot != A or q in early:
                copy(slot, q).start()
            if q == 0:
                ids_copy(slot).start()
    fill_ids(OWN)
    row_max[...] = jnp.full_like(row_max, FLOOR)
    col_max[...] = jnp.full_like(col_max, FLOOR)

    for action, slot, q in ORDER:
        if action == PASS:
            pass_on(slot, q)
        elif action == SEND:
            copy(slot, q).start()
        else:
            multiply(slot, q)

    def finish(slot):
        for j in range(rows // 128):
            window = pl.ds(128 * j, 128)
            across_rows = jnp.max(row_max[slot, window, :].T, axis=0, keepdims=True)
            back[slot, :, window] = jnp.maximum(across_rows, jnp.max(col_max[slot, :, window], axis=0, keepdims=True))

    for slot in HELD:
        finish(slot)
        back_copy(slot).start()
    finish(OWN)
    best = back[OWN]
    for slot in HELD:
        back_copy(slot).wait_recv()
        best = jnp.maximum(best, got[slot])
    best_ref[...] = best.reshape(rows)

    own = col_ids[OWN, 0:1, :]
    lane = lax.broadcasted_iota(jnp.int32, (1, 128), 1)
    partial = jnp.zeros((1, 128), jnp.float32)
    for c in range(CL_GRP):
        member = own == jnp.float32(c)
        amount = jnp.sum(jnp.where(member, best, 0.0), axis=1, keepdims=True)
        number = jnp.sum(member.astype(jnp.float32), axis=1, keepdims=True)
        partial = partial + jnp.where(lane == base + c, amount, 0.0) + jnp.where(lane == base + c + 64, number, 0.0)

    def exchange(buffer, value, me, partners, send, recv):
        buffer[me] = value
        copies = []
        for i, device in enumerate(partners):
            copies.append(pltpu.make_async_remote_copy(
                src_ref=buffer.at[me], dst_ref=buffer.at[me], send_sem=send.at[i], recv_sem=recv.at[i],
                device_id=device, device_id_type=MESH))
            copies[-1].start()
        for c in copies:
            c.wait_recv()
        return functools.reduce(jnp.add, [buffer[i] for i in range(len(partners) + 1)]), copies

    part, first = exchange(sums, partial, x * 4 + y, [in_plane(*p) for p in plane], sum_send, sum_recv)
    whole, second = exchange(total, part, z * 4 + grp, [over(*a) for a in across], tot_send, tot_recv)
    mean = whole / jnp.concatenate([whole[:, 64:], whole[:, :64]], axis=1)
    mean_ref[...] = mean.reshape(128)[:mean_ref.shape[0]]

    for slot in LINKS:
        for q in range(pieces):
            copy(slot, q).wait_send()
        ids_copy(slot).wait_send()
    for slot in HELD:
        back_copy(slot).wait_send()
    for c in first + second:
        c.wait_send()


def per_device(embeddings, cluster_ids):
    rows, width = embeddings.shape
    pieces = rows // PIECE
    dma = pltpu.SemaphoreType.DMA
    hbm = pl.BlockSpec(memory_space=pltpu.HBM)
    vmem = pl.BlockSpec(memory_space=pltpu.VMEM)
    return pl.pallas_call(
        kernel,
        out_shape=(jax.ShapeDtypeStruct((rows,), jnp.float32),
                   jax.ShapeDtypeStruct((CL_GRP * lax.axis_size("grp"),), jnp.float32)),
        in_specs=[hbm, hbm],
        out_specs=(vmem, vmem),
        scratch_shapes=[
            pltpu.VMEM((rows, width), jnp.bfloat16),
            pltpu.VMEM((rows,), jnp.int32),
            pltpu.VMEM((8, rows, width), jnp.bfloat16),
            pltpu.VMEM((7, rows, 128), jnp.float32),
            pltpu.VMEM((7, 8, rows), jnp.float32),
            pltpu.VMEM((7, rows, 128), jnp.float32),
            pltpu.VMEM((7, 8, rows), jnp.float32),
            pltpu.VMEM((8, 8, 128), jnp.float32),
            pltpu.VMEM((7, 1, rows), jnp.float32),
            pltpu.VMEM((7, 1, rows), jnp.float32),
            pltpu.VMEM((16, 1, 128), jnp.float32),
            pltpu.VMEM((8, 1, 128), jnp.float32),
            dma((pieces + 1,)),
            dma((7, pieces)), dma((7, pieces)),
            dma((7,)), dma((7,)),
            dma((6,)), dma((6,)),
            dma((15,)), dma((15,)),
            dma((7,)), dma((7,)),
        ],
        compiler_params=pltpu.CompilerParams(collective_id=0, has_side_effects=True, vmem_limit_bytes=63 * 2**20),
    )(embeddings, cluster_ids)


def solution(mesh):
    placed = (P(("grp", "blk"), None), P(("grp", "blk")))
    return jax.shard_map(
        per_device, mesh=mesh, in_specs=placed, out_specs=(P(("grp", "blk")), P()), check_vma=False
    )
```

```python
import functools

import jax
import jax.numpy as jnp
from jax import lax
from jax.experimental import pallas as pl
from jax.experimental.pallas import tpu as pltpu
from jax.sharding import PartitionSpec as P

MESH = pl.DeviceIdType.MESH
CL_GRP = 3
FLOOR = -4.0
PIECE = 128
TILE = 256

OWN, B, C, F, G, A, E, RELAY = range(8)
HELD = {B: (1, 0, 0), C: (1, 1, 0), F: (0, 3, 1), G: (3, 0, 1), A: (3, 0, 0), E: (1, 2, 0)}
LINKS = {
    A: (OWN, (1, 0, 0)),
    B: (OWN, (3, 0, 0)),
    C: (B, (0, 3, 0)),
    E: (C, (0, 3, 0)),
    RELAY: (OWN, (0, 0, 1)),
    F: (RELAY, (0, 1, 0)),
    G: (RELAY, (1, 0, 0)),
}
WHOLE = ((B, OWN), (C, OWN), (C, B), (A, C), (F, OWN), (F, B), (F, C), (G, OWN), (G, B), (G, C), (G, F), (E, OWN))
HALVED = ((A, B), (A, F), (A, G), (E, B), (E, F), (E, G), (E, A))
PASS, SEND, TILE_OF = range(3)
ORDER = (
    (PASS, B, 0),
    (PASS, B, 1),
    (TILE_OF, A, 0),
    (TILE_OF, B, 0),
    (PASS, RELAY, 0),
    (PASS, B, 2),
    (TILE_OF, A, 1),
    (PASS, RELAY, 1),
    (PASS, B, 3),
    (PASS, C, 0),
    (TILE_OF, B, 1),
    (PASS, RELAY, 2),
    (PASS, C, 1),
    (TILE_OF, C, 0),
    (PASS, B, 4),
    (TILE_OF, G, 0),
    (PASS, RELAY, 3),
    (TILE_OF, F, 0),
    (PASS, C, 2),
    (PASS, B, 5),
    (PASS, RELAY, 4),
    (TILE_OF, B, 2),
    (PASS, C, 3),
    (TILE_OF, C, 1),
    (PASS, RELAY, 5),
    (SEND, A, 4),
    (SEND, A, 5),
    (TILE_OF, E, 0),
    (TILE_OF, G, 1),
    (PASS, C, 4),
    (TILE_OF, F, 1),
    (PASS, C, 5),
    (TILE_OF, C, 2),
    (TILE_OF, E, 1),
    (TILE_OF, F, 2),
    (TILE_OF, G, 2),
    (TILE_OF, A, 2),
    (TILE_OF, E, 2),
)


def kernel(x_hbm, ids_hbm, best_ref, mean_ref, x_ref, ids_ref, held, row_max, col_max, row_ids, col_ids, counts, back, got,
           sums, total, x_sem, send_sem, recv_sem, ids_send, ids_recv, back_send, back_recv, sum_send, sum_recv, tot_send,
           tot_recv, arrived):
    rows, width = x_ref.shape
    pieces, tiles = rows // PIECE, rows // TILE
    grp, blk = lax.axis_index("grp"), lax.axis_index("blk")
    x, y, z = blk // 8, (blk // 2) % 4, blk % 2
    swap = (z + grp) % 2

    def load(q):
        window = pl.ds(q * PIECE, PIECE)
        return pltpu.make_async_copy(x_hbm.at[window], x_ref.at[window], x_sem.at[q])

    load_ids = pltpu.make_async_copy(ids_hbm, ids_ref, x_sem.at[pieces])
    for q in range(pieces):
        load(q).start()
    load_ids.start()

    def place(nx, ny, nz):
        return (lax.rem(nx + 8, 4) * 4 + lax.rem(ny + 8, 4)) * 2 + lax.rem(nz, 2)

    def times(step):
        dx, dy, dz = step
        return (grp, place(x + dx * (1 - swap) + dy * swap, y + dy * (1 - swap) + dx * swap, z + dz))

    def in_plane(dx, dy):
        return (grp, place(x + dx, y + dy, z))

    def over(dz, dl, dc):
        return (lax.rem(grp // 2 + dl, 2) * 2 + lax.rem(grp + dc, 2), place(x, y, z + dz))

    plane = [(dx, dy) for dx in range(4) for dy in range(4) if dx or dy]
    plane.sort(key=lambda p: -sum(min(d, 4 - d) for d in p))
    same_core = [(1, 0, 0), (0, 1, 0), (1, 1, 0)]
    other_core = [(1, 0, 1), (0, 1, 1), (1, 1, 1), (0, 0, 1)]

    barrier = pltpu.get_barrier_semaphore()
    greeted = [over(*a) for a in same_core] + [in_plane(*p) for p in ((0, 1), (0, 3), (1, 0), (3, 0))] + [over(0, 0, 1)]
    for device in greeted:
        pl.semaphore_signal(barrier, inc=1, device_id=device, device_id_type=MESH)

    def copy(slot, q):
        source, step = LINKS[slot]
        window = pl.ds(q * PIECE, PIECE)
        return pltpu.make_async_remote_copy(
            src_ref=held.at[source, window], dst_ref=held.at[slot, window], send_sem=send_sem.at[slot - 1, q],
            recv_sem=recv_sem.at[slot - 1, q], device_id=times(step), device_id_type=MESH)

    def ids_copy(slot):
        source, step = LINKS[slot]
        return pltpu.make_async_remote_copy(
            src_ref=counts.at[source], dst_ref=counts.at[slot], send_sem=ids_send.at[slot - 1],
            recv_sem=ids_recv.at[slot - 1], device_id=times(step), device_id_type=MESH)

    def back_copy(slot):
        return pltpu.make_async_remote_copy(
            src_ref=back.at[slot], dst_ref=got.at[slot], send_sem=back_send.at[slot - 1],
            recv_sem=back_recv.at[slot - 1], device_id=times(HELD[slot]), device_id_type=MESH)

    def normalise(q):
        load(q).wait()
        window = pl.ds(q * PIECE, PIECE)
        wide = x_ref[window, :].astype(jnp.float32)
        norms = jnp.sum(wide * wide, axis=1, keepdims=True)
        held[OWN, window, :] = (wide * lax.rsqrt(norms + 1e-06)).astype(jnp.bfloat16)

    def fill_ids(slot):
        low, high = counts[slot, 0:1, :], counts[slot, 1:2, :]
        at = lax.broadcasted_iota(jnp.int32, (rows, 128), 0).astype(jnp.float32)
        row_ids[slot] = (at >= low).astype(jnp.float32) + (at >= high).astype(jnp.float32)
        for j in range(rows // 128):
            at = (lax.broadcasted_iota(jnp.int32, (8, 128), 1) + 128 * j).astype(jnp.float32)
            col_ids[slot, :, pl.ds(128 * j, 128)] = (at >= low).astype(jnp.float32) + (at >= high).astype(jnp.float32)

    def product(j, first, n, s, q, diagonal=False):
        window = pl.ds(q * TILE, TILE)
        scores = lax.dot_general(held[j, pl.ds(first, n), :], held[s, window, :], (((1,), (1,)), ((), ())),
                                 preferred_element_type=jnp.float32)
        ids = row_ids[j, pl.ds(first, n), :]
        same = jnp.concatenate([ids] * (TILE // 128), axis=1) == col_ids[s, 0:1, window]
        if diagonal:
            same = same & (lax.broadcasted_iota(jnp.int32, (n, TILE), 0) != lax.broadcasted_iota(jnp.int32, (n, TILE), 1))
        masked = jnp.where(same, scores, jnp.float32(FLOOR))
        across_tile = functools.reduce(jnp.maximum, [masked[:, 128 * t:128 * t + 128] for t in range(TILE // 128)])
        row_max[j, pl.ds(first, n), :] = jnp.maximum(row_max[j, pl.ds(first, n), :], across_tile)
        if not diagonal:
            down = jnp.max(masked.reshape(n // 8, 8, TILE), axis=0)
            col_max[s, :, window] = jnp.maximum(col_max[s, :, window], down)

    waited, ready, tiles_in = set(), set(), set()

    def wait(slot, q):
        if (slot, q) not in waited:
            waited.add((slot, q))
            copy(slot, q).wait_recv()

    def wait_ids(slot):
        if slot not in ready:
            ready.add(slot)
            ids_copy(slot).wait_recv()
            if slot != RELAY:
                fill_ids(slot)

    def wanted(s, q, j, r):
        if (s, j) in WHOLE or (j, s) in WHOLE:
            return True
        return ((s, j) in HALVED and r >= q) or ((j, s) in HALVED and q >= r)

    def multiply(s, q):
        tiles_in.add((s, q))
        if s == OWN:
            product(OWN, q * TILE, TILE, OWN, q, diagonal=True)
            if q + 1 < tiles:
                product(OWN, (q + 1) * TILE, rows - (q + 1) * TILE, OWN, q)
            return
        for p in range(q * TILE // PIECE, (q + 1) * TILE // PIECE):
            wait(s, p)
        wait_ids(s)
        for j in (OWN, *HELD):
            if j == s:
                continue
            r = 0
            while r < tiles:
                end = r
                while end < tiles and (j, end) in tiles_in and wanted(s, q, j, end):
                    end += 1
                if end > r:
                    product(j, r * TILE, (end - r) * TILE, s, q)
                r = end + 1

    def pass_on(slot, q):
        wait(slot, q)
        onward = [to for to, (source, _) in LINKS.items() if source == slot]
        for to in onward:
            copy(to, q).start()
        if q == 0:
            wait_ids(slot)
            for to in onward:
                ids_copy(to).start()

    load_ids.wait()
    ids = ids_ref[...].reshape(1, rows)
    base = grp * CL_GRP
    low = jnp.sum((ids <= base).astype(jnp.float32), axis=1, keepdims=True)
    high = jnp.sum((ids <= base + 1).astype(jnp.float32), axis=1, keepdims=True)
    counts[OWN] = jnp.where(lax.broadcasted_iota(jnp.int32, (8, 128), 0) == 0, low, high)

    for q in range(pieces):
        normalise(q)
    fill_ids(OWN)
    row_max[...] = jnp.full_like(row_max, FLOOR)
    col_max[...] = jnp.full_like(col_max, FLOOR)
    for q in range(tiles):
        multiply(OWN, q)

    pl.semaphore_wait(barrier, len(greeted))
    early = [q for q in range(pieces) if (SEND, A, q) not in ORDER]
    for q in range(pieces):
        for slot in (B, RELAY, A):
            if slot != A or q in early:
                copy(slot, q).start()
            if q == 0:
                ids_copy(slot).start()
    for a in same_core:
        pl.semaphore_signal(arrived, inc=1, device_id=over(*a), device_id_type=MESH)
    relative = col_ids[OWN, 0:1, :]
    sublane = lax.broadcasted_iota(jnp.int32, (8, 1), 0)
    lane = lax.broadcasted_iota(jnp.int32, (8, 128), 1)
    member = relative == sublane.astype(jnp.float32)
    number = jnp.sum(member.astype(jnp.float32), axis=1, keepdims=True)
    here = lane == base + sublane
    numbers = jnp.sum(jnp.where((lane == base + sublane + 64) & (sublane < CL_GRP), number, 0.0), axis=0, keepdims=True)

    for action, slot, q in ORDER:
        if action == PASS:
            pass_on(slot, q)
        elif action == SEND:
            copy(slot, q).start()
        else:
            multiply(slot, q)

    def finish(slot):
        for j in range(rows // 128):
            window = pl.ds(128 * j, 128)
            across_rows = jnp.max(row_max[slot, window, :].T, axis=0, keepdims=True)
            back[slot, :, window] = jnp.maximum(across_rows, jnp.max(col_max[slot, :, window], axis=0, keepdims=True))

    for slot in (E, F, G, C, A, B):
        finish(slot)
        back_copy(slot).start()
    finish(OWN)
    for slot in LINKS:
        for q in range(pieces):
            copy(slot, q).wait_send()
        ids_copy(slot).wait_send()
    pl.semaphore_wait(arrived, len(same_core))
    best = back[OWN]
    for slot in HELD:
        back_copy(slot).wait_recv()
        best = jnp.maximum(best, got[slot])

    amount = jnp.sum(jnp.where(member, best, 0.0), axis=1, keepdims=True)
    partial = numbers + jnp.sum(jnp.where(here & (sublane < CL_GRP), amount, 0.0), axis=0, keepdims=True)

    def exchange(buffer, value, me, partners, send, recv):
        buffer[me] = value
        copies = []
        for i, device in enumerate(partners):
            copies.append(pltpu.make_async_remote_copy(
                src_ref=buffer.at[me], dst_ref=buffer.at[me], send_sem=send.at[i], recv_sem=recv.at[i],
                device_id=device, device_id_type=MESH))
            copies[-1].start()
        return copies

    def total_of(buffer, copies):
        for c in copies:
            c.wait_recv()
        return functools.reduce(jnp.add, [buffer[i] for i in range(len(copies) + 1)])

    first = exchange(sums, partial, x * 4 + y, [in_plane(*p) for p in plane], sum_send, sum_recv)
    best_ref[...] = best.reshape(rows)
    for slot in HELD:
        back_copy(slot).wait_send()
    part = total_of(sums, first)
    second = exchange(total, part, z * 4 + grp, [over(*a) for a in same_core + other_core], tot_send, tot_recv)
    for c in first:
        c.wait_send()
    whole = total_of(total, second)
    mean = whole / jnp.concatenate([whole[:, 64:], whole[:, :64]], axis=1)
    mean_ref[...] = mean.reshape(128)[:mean_ref.shape[0]]
    for c in second:
        c.wait_send()


def per_device(embeddings, cluster_ids):
    rows, width = embeddings.shape
    pieces = rows // PIECE
    dma = pltpu.SemaphoreType.DMA
    hbm = pl.BlockSpec(memory_space=pltpu.HBM)
    vmem = pl.BlockSpec(memory_space=pltpu.VMEM)
    return pl.pallas_call(
        kernel,
        out_shape=(jax.ShapeDtypeStruct((rows,), jnp.float32),
                   jax.ShapeDtypeStruct((CL_GRP * lax.axis_size("grp"),), jnp.float32)),
        in_specs=[hbm, hbm],
        out_specs=(vmem, vmem),
        scratch_shapes=[
            pltpu.VMEM((rows, width), jnp.bfloat16),
            pltpu.VMEM((rows,), jnp.int32),
            pltpu.VMEM((8, rows, width), jnp.bfloat16),
            pltpu.VMEM((7, rows, 128), jnp.float32),
            pltpu.VMEM((7, 8, rows), jnp.float32),
            pltpu.VMEM((7, rows, 128), jnp.float32),
            pltpu.VMEM((7, 8, rows), jnp.float32),
            pltpu.VMEM((8, 8, 128), jnp.float32),
            pltpu.VMEM((7, 1, rows), jnp.float32),
            pltpu.VMEM((7, 1, rows), jnp.float32),
            pltpu.VMEM((16, 1, 128), jnp.float32),
            pltpu.VMEM((8, 1, 128), jnp.float32),
            dma((pieces + 1,)),
            dma((7, pieces)), dma((7, pieces)),
            dma((7,)), dma((7,)),
            dma((6,)), dma((6,)),
            dma((15,)), dma((15,)),
            dma((7,)), dma((7,)),
            pltpu.SemaphoreType.REGULAR,
        ],
        compiler_params=pltpu.CompilerParams(collective_id=0, has_side_effects=True, vmem_limit_bytes=107 * 2**19),
    )(embeddings, cluster_ids)


def solution(mesh):
    placed = (P(("grp", "blk"), None), P(("grp", "blk")))
    return jax.shard_map(
        per_device, mesh=mesh, in_specs=placed, out_specs=(P(("grp", "blk")), P()), check_vma=False
    )
```

```python
import functools

import jax
import jax.numpy as jnp
from jax import lax
from jax.experimental import pallas as pl
from jax.experimental.pallas import tpu as pltpu
from jax.sharding import PartitionSpec as P

MESH = pl.DeviceIdType.MESH
CL_GRP = 3
FLOOR = -4.0
PIECE = 128
TILE = 256

OWN, B, C, F, G, A, E, RELAY = range(8)
HELD = {B: (1, 0, 0), C: (1, 1, 0), F: (0, 3, 1), G: (3, 0, 1), A: (3, 0, 0), E: (1, 2, 0)}
LINKS = {
    A: (OWN, (1, 0, 0)),
    B: (OWN, (3, 0, 0)),
    C: (B, (0, 3, 0)),
    E: (C, (0, 3, 0)),
    RELAY: (OWN, (0, 0, 1)),
    F: (RELAY, (0, 1, 0)),
    G: (RELAY, (1, 0, 0)),
}
LATE_F = 0


def link(slot, q, pieces):
    if slot == F and q >= pieces - LATE_F:
        return A, (0, 0, 1)
    return LINKS[slot]


WHOLE = ((B, OWN), (C, OWN), (C, B), (A, C), (F, OWN), (F, B), (F, C), (G, OWN), (G, B), (G, C), (G, F), (E, OWN))
HALVED = ((A, B), (A, F), (A, G), (E, B), (E, F), (E, G), (E, A))
PASS, SEND, TILE_OF = range(3)
ORDER = (
    (PASS, B, 0),
    (TILE_OF, A, 0),
    (PASS, RELAY, 0),
    (PASS, RELAY, 1),
    (PASS, B, 1),
    (PASS, B, 2),
    (PASS, B, 3),
    (TILE_OF, B, 0),
    (PASS, RELAY, 2),
    (TILE_OF, A, 1),
    (PASS, C, 0),
    (PASS, RELAY, 3),
    (PASS, B, 4),
    (PASS, B, 5),
    (TILE_OF, B, 2),
    (TILE_OF, B, 1),
    (TILE_OF, C, 0),
    (PASS, RELAY, 4),
    (PASS, C, 1),
    (PASS, C, 2),
    (TILE_OF, A, 2),
    (TILE_OF, F, 0),
    (TILE_OF, C, 1),
    (TILE_OF, G, 0),
    (PASS, C, 3),
    (PASS, C, 4),
    (PASS, RELAY, 5),
    (PASS, C, 5),
    (TILE_OF, F, 1),
    (TILE_OF, C, 2),
    (TILE_OF, E, 0),
    (TILE_OF, G, 1),
    (TILE_OF, E, 1),
    (TILE_OF, F, 2),
    (TILE_OF, E, 2),
    (TILE_OF, G, 2),
)


def kernel(x_hbm, ids_hbm, best_ref, mean_ref, x_ref, ids_ref, held, row_max, col_max, row_ids, col_ids, counts, back, got,
           sums, total, x_sem, send_sem, recv_sem, ids_send, ids_recv, back_send, back_recv, sum_send, sum_recv, tot_send,
           tot_recv, arrived):
    rows, width = x_ref.shape
    pieces, tiles = rows // PIECE, rows // TILE
    grp, blk = lax.axis_index("grp"), lax.axis_index("blk")
    x, y, z = blk // 8, (blk // 2) % 4, blk % 2
    swap = (z + grp) % 2

    def load(q):
        window = pl.ds(q * PIECE, PIECE)
        return pltpu.make_async_copy(x_hbm.at[window], x_ref.at[window], x_sem.at[q])

    load_ids = pltpu.make_async_copy(ids_hbm, ids_ref, x_sem.at[pieces])
    for q in range(pieces):
        load(q).start()
    load_ids.start()

    def place(nx, ny, nz):
        return (lax.rem(nx + 8, 4) * 4 + lax.rem(ny + 8, 4)) * 2 + lax.rem(nz, 2)

    def times(step):
        dx, dy, dz = step
        return (grp, place(x + dx * (1 - swap) + dy * swap, y + dy * (1 - swap) + dx * swap, z + dz))

    def in_plane(dx, dy):
        return (grp, place(x + dx, y + dy, z))

    def over(dz, dl, dc):
        return (lax.rem(grp // 2 + dl, 2) * 2 + lax.rem(grp + dc, 2), place(x, y, z + dz))

    plane = [(dx, dy) for dx in range(4) for dy in range(4) if dx or dy]
    plane.sort(key=lambda p: -sum(min(d, 4 - d) for d in p))
    same_core = [(1, 0, 0), (0, 1, 0), (1, 1, 0)]
    other_core = [(1, 0, 1), (0, 1, 1), (1, 1, 1), (0, 0, 1)]

    barrier = pltpu.get_barrier_semaphore()
    greeted = [over(*a) for a in same_core] + [in_plane(*p) for p in ((0, 1), (0, 3), (1, 0), (3, 0))] + [over(0, 0, 1)]
    for device in greeted:
        pl.semaphore_signal(barrier, inc=1, device_id=device, device_id_type=MESH)

    def copy(slot, q):
        source, step = link(slot, q, pieces)
        window = pl.ds(q * PIECE, PIECE)
        return pltpu.make_async_remote_copy(
            src_ref=held.at[source, window], dst_ref=held.at[slot, window], send_sem=send_sem.at[slot - 1, q],
            recv_sem=recv_sem.at[slot - 1, q], device_id=times(step), device_id_type=MESH)

    def ids_copy(slot):
        source, step = LINKS[slot]
        return pltpu.make_async_remote_copy(
            src_ref=counts.at[source], dst_ref=counts.at[slot], send_sem=ids_send.at[slot - 1],
            recv_sem=ids_recv.at[slot - 1], device_id=times(step), device_id_type=MESH)

    def back_copy(slot):
        return pltpu.make_async_remote_copy(
            src_ref=back.at[slot], dst_ref=got.at[slot], send_sem=back_send.at[slot - 1],
            recv_sem=back_recv.at[slot - 1], device_id=times(HELD[slot]), device_id_type=MESH)

    def normalise(q):
        load(q).wait()
        window = pl.ds(q * PIECE, PIECE)
        wide = x_ref[window, :].astype(jnp.float32)
        norms = jnp.sum(wide * wide, axis=1, keepdims=True)
        held[OWN, window, :] = (wide * lax.rsqrt(norms + 1e-06)).astype(jnp.bfloat16)

    def fill_ids(slot):
        low, high = counts[slot, 0:1, :], counts[slot, 1:2, :]
        at = lax.broadcasted_iota(jnp.int32, (rows, 128), 0).astype(jnp.float32)
        row_ids[slot] = (at >= low).astype(jnp.float32) + (at >= high).astype(jnp.float32)
        for j in range(rows // 128):
            at = (lax.broadcasted_iota(jnp.int32, (8, 128), 1) + 128 * j).astype(jnp.float32)
            col_ids[slot, :, pl.ds(128 * j, 128)] = (at >= low).astype(jnp.float32) + (at >= high).astype(jnp.float32)

    def product(j, first, n, s, q, diagonal=False):
        window = pl.ds(q * TILE, TILE)
        scores = lax.dot_general(held[j, pl.ds(first, n), :], held[s, window, :], (((1,), (1,)), ((), ())),
                                 preferred_element_type=jnp.float32)
        ids = row_ids[j, pl.ds(first, n), :]
        same = jnp.concatenate([ids] * (TILE // 128), axis=1) == col_ids[s, 0:1, window]
        if diagonal:
            same = same & (lax.broadcasted_iota(jnp.int32, (n, TILE), 0) != lax.broadcasted_iota(jnp.int32, (n, TILE), 1))
        masked = jnp.where(same, scores, jnp.float32(FLOOR))
        across_tile = functools.reduce(jnp.maximum, [masked[:, 128 * t:128 * t + 128] for t in range(TILE // 128)])
        row_max[j, pl.ds(first, n), :] = jnp.maximum(row_max[j, pl.ds(first, n), :], across_tile)
        if not diagonal:
            down = jnp.max(masked.reshape(n // 8, 8, TILE), axis=0)
            col_max[s, :, window] = jnp.maximum(col_max[s, :, window], down)

    waited, ready, tiles_in = set(), set(), set()

    def wait(slot, q):
        if (slot, q) not in waited:
            waited.add((slot, q))
            copy(slot, q).wait_recv()

    def wait_ids(slot):
        if slot not in ready:
            ready.add(slot)
            ids_copy(slot).wait_recv()
            if slot != RELAY:
                fill_ids(slot)

    def wanted(s, q, j, r):
        if (s, j) in WHOLE or (j, s) in WHOLE:
            return True
        return ((s, j) in HALVED and r >= q) or ((j, s) in HALVED and q >= r)

    def multiply(s, q):
        tiles_in.add((s, q))
        if s == OWN:
            product(OWN, q * TILE, TILE, OWN, q, diagonal=True)
            if q + 1 < tiles:
                product(OWN, (q + 1) * TILE, rows - (q + 1) * TILE, OWN, q)
            return
        for p in range(q * TILE // PIECE, (q + 1) * TILE // PIECE):
            wait(s, p)
        wait_ids(s)
        for j in (OWN, *HELD):
            if j == s:
                continue
            r = 0
            while r < tiles:
                end = r
                while end < tiles and (j, end) in tiles_in and wanted(s, q, j, end):
                    end += 1
                if end > r:
                    product(j, r * TILE, (end - r) * TILE, s, q)
                r = end + 1

    def pass_on(slot, q):
        wait(slot, q)
        for to in LINKS:
            if link(to, q, pieces)[0] == slot:
                copy(to, q).start()
        if q == 0:
            wait_ids(slot)
            for to, (source, _) in LINKS.items():
                if source == slot:
                    ids_copy(to).start()

    load_ids.wait()
    ids = ids_ref[...].reshape(1, rows)
    base = grp * CL_GRP
    low = jnp.sum((ids <= base).astype(jnp.float32), axis=1, keepdims=True)
    high = jnp.sum((ids <= base + 1).astype(jnp.float32), axis=1, keepdims=True)
    counts[OWN] = jnp.where(lax.broadcasted_iota(jnp.int32, (8, 128), 0) == 0, low, high)

    for q in range(pieces):
        normalise(q)
    fill_ids(OWN)
    row_max[...] = jnp.full_like(row_max, FLOOR)
    col_max[...] = jnp.full_like(col_max, FLOOR)
    for q in range(tiles):
        multiply(OWN, q)

    pl.semaphore_wait(barrier, len(greeted))
    early = [q for q in range(pieces) if (SEND, A, q) not in ORDER]
    for q in range(pieces):
        for slot in (B, RELAY, A):
            if slot != A or q in early:
                copy(slot, q).start()
            if q == 0:
                ids_copy(slot).start()
    for a in same_core:
        pl.semaphore_signal(arrived, inc=1, device_id=over(*a), device_id_type=MESH)
    relative = col_ids[OWN, 0:1, :]
    sublane = lax.broadcasted_iota(jnp.int32, (8, 1), 0)
    lane = lax.broadcasted_iota(jnp.int32, (8, 128), 1)
    member = relative == sublane.astype(jnp.float32)
    number = jnp.sum(member.astype(jnp.float32), axis=1, keepdims=True)
    here = lane == base + sublane
    numbers = jnp.sum(jnp.where((lane == base + sublane + 64) & (sublane < CL_GRP), number, 0.0), axis=0, keepdims=True)

    for action, slot, q in ORDER:
        if action == PASS:
            pass_on(slot, q)
        elif action == SEND:
            copy(slot, q).start()
        else:
            multiply(slot, q)

    def finish(slot):
        for j in range(rows // 128):
            window = pl.ds(128 * j, 128)
            across_rows = jnp.max(row_max[slot, window, :].T, axis=0, keepdims=True)
            back[slot, :, window] = jnp.maximum(across_rows, jnp.max(col_max[slot, :, window], axis=0, keepdims=True))

    for slot in (E, F, G, C, A, B):
        finish(slot)
        back_copy(slot).start()
    finish(OWN)
    for slot in LINKS:
        for q in range(pieces):
            copy(slot, q).wait_send()
        ids_copy(slot).wait_send()
    pl.semaphore_wait(arrived, len(same_core))
    best = back[OWN]
    for slot in HELD:
        back_copy(slot).wait_recv()
        best = jnp.maximum(best, got[slot])

    amount = jnp.sum(jnp.where(member, best, 0.0), axis=1, keepdims=True)
    partial = numbers + jnp.sum(jnp.where(here & (sublane < CL_GRP), amount, 0.0), axis=0, keepdims=True)

    def exchange(buffer, value, me, partners, send, recv):
        buffer[me] = value
        copies = []
        for i, device in enumerate(partners):
            copies.append(pltpu.make_async_remote_copy(
                src_ref=buffer.at[me], dst_ref=buffer.at[me], send_sem=send.at[i], recv_sem=recv.at[i],
                device_id=device, device_id_type=MESH))
            copies[-1].start()
        return copies

    def total_of(buffer, copies):
        for c in copies:
            c.wait_recv()
        return functools.reduce(jnp.add, [buffer[i] for i in range(len(copies) + 1)])

    first = exchange(sums, partial, x * 4 + y, [in_plane(*p) for p in plane], sum_send, sum_recv)
    best_ref[...] = best.reshape(rows)
    for slot in HELD:
        back_copy(slot).wait_send()
    part = total_of(sums, first)
    second = exchange(total, part, z * 4 + grp, [over(*a) for a in same_core + other_core], tot_send, tot_recv)
    for c in first:
        c.wait_send()
    whole = total_of(total, second)
    mean = whole / jnp.concatenate([whole[:, 64:], whole[:, :64]], axis=1)
    mean_ref[...] = mean.reshape(128)[:mean_ref.shape[0]]
    for c in second:
        c.wait_send()


def per_device(embeddings, cluster_ids):
    rows, width = embeddings.shape
    pieces = rows // PIECE
    dma = pltpu.SemaphoreType.DMA
    hbm = pl.BlockSpec(memory_space=pltpu.HBM)
    vmem = pl.BlockSpec(memory_space=pltpu.VMEM)
    return pl.pallas_call(
        kernel,
        out_shape=(jax.ShapeDtypeStruct((rows,), jnp.float32),
                   jax.ShapeDtypeStruct((CL_GRP * lax.axis_size("grp"),), jnp.float32)),
        in_specs=[hbm, hbm],
        out_specs=(vmem, vmem),
        scratch_shapes=[
            pltpu.VMEM((rows, width), jnp.bfloat16),
            pltpu.VMEM((rows,), jnp.int32),
            pltpu.VMEM((8, rows, width), jnp.bfloat16),
            pltpu.VMEM((7, rows, 128), jnp.float32),
            pltpu.VMEM((7, 8, rows), jnp.float32),
            pltpu.VMEM((7, rows, 128), jnp.float32),
            pltpu.VMEM((7, 8, rows), jnp.float32),
            pltpu.VMEM((8, 8, 128), jnp.float32),
            pltpu.VMEM((7, 1, rows), jnp.float32),
            pltpu.VMEM((7, 1, rows), jnp.float32),
            pltpu.VMEM((16, 1, 128), jnp.float32),
            pltpu.VMEM((8, 1, 128), jnp.float32),
            dma((pieces + 1,)),
            dma((7, pieces)), dma((7, pieces)),
            dma((7,)), dma((7,)),
            dma((6,)), dma((6,)),
            dma((15,)), dma((15,)),
            dma((7,)), dma((7,)),
            pltpu.SemaphoreType.REGULAR,
        ],
        compiler_params=pltpu.CompilerParams(collective_id=0, has_side_effects=True, vmem_limit_bytes=863 * 2**16 - 2**13),
    )(embeddings, cluster_ids)


def solution(mesh):
    placed = (P(("grp", "blk"), None), P(("grp", "blk")))
    return jax.shard_map(
        per_device, mesh=mesh, in_specs=placed, out_specs=(P(("grp", "blk")), P()), check_vma=False
    )
```

```python
import functools

import jax
import jax.numpy as jnp
from jax import lax
from jax.experimental import pallas as pl
from jax.experimental.pallas import tpu as pltpu
from jax.sharding import PartitionSpec as P

MESH = pl.DeviceIdType.MESH
CL_GRP = 3
FLOOR = -4.0
PIECE = 128
TILE = 256

OWN, B, C, F, G, A, E, RELAY = range(8)
HELD = {B: (1, 0, 0), C: (1, 1, 0), F: (0, 3, 1), G: (3, 0, 1), A: (3, 0, 0), E: (1, 2, 0)}
LINKS = {
    A: (OWN, (1, 0, 0)),
    B: (OWN, (3, 0, 0)),
    C: (B, (0, 3, 0)),
    E: (C, (0, 3, 0)),
    RELAY: (OWN, (0, 0, 1)),
    F: (RELAY, (0, 1, 0)),
    G: (RELAY, (1, 0, 0)),
}
WHOLE = ((B, OWN), (C, OWN), (C, B), (A, C), (F, OWN), (F, B), (F, C), (G, OWN), (G, B), (G, C), (G, F), (E, OWN))
HALVED = ((A, B), (A, F), (A, G), (E, B), (E, F), (E, G), (E, A))
PASS, SEND, TILE_OF, CUT = range(4)
ORDER = (
    (PASS, RELAY, 0),
    (TILE_OF, B, 0),
    (PASS, B, 0),
    (TILE_OF, B, 1),
    (PASS, B, 1),
    (PASS, B, 2),
    (PASS, RELAY, 1),
    (PASS, RELAY, 2),
    (PASS, B, 3),
    (PASS, C, 0),
    (PASS, C, 1),
    (PASS, B, 4),
    (TILE_OF, A, 0),
    (PASS, RELAY, 3),
    (TILE_OF, G, 0),
    (TILE_OF, F, 0),
    (PASS, B, 5),
    (PASS, C, 2),
    (PASS, RELAY, 4),
    (TILE_OF, C, 1),
    (TILE_OF, A, 1),
    (TILE_OF, B, 2),
    (TILE_OF, C, 0),
    (PASS, RELAY, 5),
    (PASS, C, 3),
    (TILE_OF, F, 1),
    (TILE_OF, E, 0),
    (SEND, A, 4),
    (SEND, A, 5),
    (PASS, C, 4),
    (PASS, C, 5),
    (TILE_OF, G, 1),
    (TILE_OF, C, 2),
    (CUT, OWN, 0),
    (TILE_OF, E, 1),
    (CUT, OWN, 0),
    (TILE_OF, G, 2),
    (TILE_OF, F, 2),
    (CUT, OWN, 0),
    (TILE_OF, E, 2),
    (TILE_OF, A, 2),
)


def kernel(x_hbm, ids_hbm, best_ref, mean_ref, x_ref, ids_ref, held, row_max, col_max, row_ids, col_ids, counts, back, got,
           sums, total, x_sem, send_sem, recv_sem, ids_send, ids_recv, back_send, back_recv, sum_send, sum_recv, tot_send,
           tot_recv, arrived):
    rows, width = x_ref.shape
    pieces, tiles = rows // PIECE, rows // TILE
    grp, blk = lax.axis_index("grp"), lax.axis_index("blk")
    x, y, z = blk // 8, (blk // 2) % 4, blk % 2
    swap = (z + grp) % 2

    def load(q):
        window = pl.ds(q * PIECE, PIECE)
        return pltpu.make_async_copy(x_hbm.at[window], x_ref.at[window], x_sem.at[q])

    load_ids = pltpu.make_async_copy(ids_hbm, ids_ref, x_sem.at[pieces])
    for q in range(pieces):
        load(q).start()
    load_ids.start()

    def place(nx, ny, nz):
        return (lax.rem(nx + 8, 4) * 4 + lax.rem(ny + 8, 4)) * 2 + lax.rem(nz, 2)

    def times(step):
        dx, dy, dz = step
        return (grp, place(x + dx * (1 - swap) + dy * swap, y + dy * (1 - swap) + dx * swap, z + dz))

    def in_plane(dx, dy):
        return (grp, place(x + dx, y + dy, z))

    def over(dz, dl, dc):
        return (lax.rem(grp // 2 + dl, 2) * 2 + lax.rem(grp + dc, 2), place(x, y, z + dz))

    plane = [(dx, dy) for dx in range(4) for dy in range(4) if dx or dy]
    plane.sort(key=lambda p: -sum(min(d, 4 - d) for d in p))
    same_core = [(1, 0, 0), (0, 1, 0), (1, 1, 0)]
    other_core = [(1, 0, 1), (0, 1, 1), (1, 1, 1), (0, 0, 1)]

    next_device = {slot: times(step) for slot, (_, step) in LINKS.items()}
    owner = {slot: times(step) for slot, step in HELD.items()}
    plane_devices = [in_plane(*p) for p in plane]
    column_devices = [over(*a) for a in same_core + other_core]

    barrier = pltpu.get_barrier_semaphore()
    greeted = [over(*a) for a in same_core] + [in_plane(*p) for p in ((0, 1), (0, 3), (1, 0), (3, 0))] + [over(0, 0, 1)]
    for device in greeted:
        pl.semaphore_signal(barrier, inc=1, device_id=device, device_id_type=MESH)

    def copy(slot, q):
        source = LINKS[slot][0]
        window = pl.ds(q * PIECE, PIECE)
        return pltpu.make_async_remote_copy(
            src_ref=held.at[source, window], dst_ref=held.at[slot, window], send_sem=send_sem.at[slot - 1, q],
            recv_sem=recv_sem.at[slot - 1, q], device_id=next_device[slot], device_id_type=MESH)

    def ids_copy(slot):
        source = LINKS[slot][0]
        return pltpu.make_async_remote_copy(
            src_ref=counts.at[source], dst_ref=counts.at[slot], send_sem=ids_send.at[slot - 1],
            recv_sem=ids_recv.at[slot - 1], device_id=next_device[slot], device_id_type=MESH)

    def back_copy(slot):
        return pltpu.make_async_remote_copy(
            src_ref=back.at[slot], dst_ref=got.at[slot], send_sem=back_send.at[slot - 1],
            recv_sem=back_recv.at[slot - 1], device_id=owner[slot], device_id_type=MESH)

    def normalise(q):
        load(q).wait()
        window = pl.ds(q * PIECE, PIECE)
        wide = x_ref[window, :].astype(jnp.float32)
        norms = jnp.sum(wide * wide, axis=1, keepdims=True)
        held[OWN, window, :] = (wide * lax.rsqrt(norms + 1e-06)).astype(jnp.bfloat16)

    def fill_ids(slot):
        low, high = counts[slot, 0:1, :], counts[slot, 1:2, :]
        at = lax.broadcasted_iota(jnp.int32, (rows, 128), 0).astype(jnp.float32)
        row_ids[slot] = (at >= low).astype(jnp.float32) + (at >= high).astype(jnp.float32)
        for j in range(rows // 128):
            at = (lax.broadcasted_iota(jnp.int32, (8, 128), 1) + 128 * j).astype(jnp.float32)
            col_ids[slot, :, pl.ds(128 * j, 128)] = (at >= low).astype(jnp.float32) + (at >= high).astype(jnp.float32)

    def product(j, first, n, s, q, diagonal=False):
        window = pl.ds(q * TILE, TILE)
        scores = lax.dot_general(held[j, pl.ds(first, n), :], held[s, window, :], (((1,), (1,)), ((), ())),
                                 preferred_element_type=jnp.float32)
        ids = row_ids[j, pl.ds(first, n), :]
        same = jnp.concatenate([ids] * (TILE // 128), axis=1) == col_ids[s, 0:1, window]
        if diagonal:
            same = same & (lax.broadcasted_iota(jnp.int32, (n, TILE), 0) != lax.broadcasted_iota(jnp.int32, (n, TILE), 1))
        masked = jnp.where(same, scores, jnp.float32(FLOOR))
        across_tile = functools.reduce(jnp.maximum, [masked[:, 128 * t:128 * t + 128] for t in range(TILE // 128)])
        row_max[j, pl.ds(first, n), :] = jnp.maximum(row_max[j, pl.ds(first, n), :], across_tile)
        if not diagonal:
            down = jnp.max(masked.reshape(n // 8, 8, TILE), axis=0)
            col_max[s, :, window] = jnp.maximum(col_max[s, :, window], down)

    waited, ready, tiles_in = set(), set(), set()

    def wait(slot, q):
        if (slot, q) not in waited:
            waited.add((slot, q))
            copy(slot, q).wait_recv()

    def wait_ids(slot):
        if slot not in ready:
            ready.add(slot)
            ids_copy(slot).wait_recv()
            if slot != RELAY:
                fill_ids(slot)

    def wait_tile(s, q):
        for p in range(q * TILE // PIECE, (q + 1) * TILE // PIECE):
            wait(s, p)
        wait_ids(s)

    def wanted(s, q, j, r):
        if (s, j) in WHOLE or (j, s) in WHOLE:
            return True
        return ((s, j) in HALVED and r >= q) or ((j, s) in HALVED and q >= r)

    def multiply(s, q):
        tiles_in.add((s, q))
        if s == OWN:
            product(OWN, q * TILE, TILE, OWN, q, diagonal=True)
            if q + 1 < tiles:
                product(OWN, (q + 1) * TILE, rows - (q + 1) * TILE, OWN, q)
            return
        wait_tile(s, q)
        for j in (OWN, *HELD):
            if j == s:
                continue
            r = 0
            while r < tiles:
                end = r
                while end < tiles and (j, end) in tiles_in and wanted(s, q, j, end):
                    end += 1
                if end > r:
                    product(j, r * TILE, (end - r) * TILE, s, q)
                r = end + 1

    def pass_on(slot, q):
        wait(slot, q)
        onward = [to for to, (source, _) in LINKS.items() if source == slot]
        for to in onward:
            copy(to, q).start()
        if q == 0:
            wait_ids(slot)
            for to in onward:
                ids_copy(to).start()

    load_ids.wait()
    ids = ids_ref[...].reshape(1, rows)
    base = grp * CL_GRP
    low = jnp.sum((ids <= base).astype(jnp.float32), axis=1, keepdims=True)
    high = jnp.sum((ids <= base + 1).astype(jnp.float32), axis=1, keepdims=True)
    counts[OWN] = jnp.where(lax.broadcasted_iota(jnp.int32, (8, 128), 0) == 0, low, high)

    for q in range(pieces):
        normalise(q)
    fill_ids(OWN)
    row_max[...] = jnp.full_like(row_max, FLOOR)
    col_max[...] = jnp.full_like(col_max, FLOOR)
    for q in range(tiles):
        multiply(OWN, q)

    pl.semaphore_wait(barrier, len(greeted))
    early = [q for q in range(pieces) if (SEND, A, q) not in ORDER]
    for q in range(pieces):
        for slot in (B, RELAY, A):
            if slot != A or q in early:
                copy(slot, q).start()
            if q == 0:
                ids_copy(slot).start()
    for a in same_core:
        pl.semaphore_signal(arrived, inc=1, device_id=over(*a), device_id_type=MESH)
    relative = col_ids[OWN, 0:1, :]
    sublane = lax.broadcasted_iota(jnp.int32, (8, 1), 0)
    lane = lax.broadcasted_iota(jnp.int32, (8, 128), 1)
    member = relative == sublane.astype(jnp.float32)
    number = jnp.sum(member.astype(jnp.float32), axis=1, keepdims=True)
    here = lane == base + sublane
    numbers = jnp.sum(jnp.where((lane == base + sublane + 64) & (sublane < CL_GRP), number, 0.0), axis=0, keepdims=True)

    for i, (action, slot, q) in enumerate(ORDER):
        if action == PASS:
            pass_on(slot, q)
        elif action == SEND:
            copy(slot, q).start()
        elif action == TILE_OF:
            for group_action, s, t in ORDER[i:]:
                if group_action != TILE_OF:
                    break
                wait_tile(s, t)
            multiply(slot, q)

    def finish(slot):
        for j in range(rows // 128):
            window = pl.ds(128 * j, 128)
            across_rows = jnp.max(row_max[slot, window, :].T, axis=0, keepdims=True)
            back[slot, :, window] = jnp.maximum(across_rows, jnp.max(col_max[slot, :, window], axis=0, keepdims=True))

    for slot in (E, F, G, C, A, B):
        finish(slot)
        back_copy(slot).start()
    finish(OWN)
    for slot in LINKS:
        for q in range(pieces):
            copy(slot, q).wait_send()
        ids_copy(slot).wait_send()
    pl.semaphore_wait(arrived, len(same_core))
    best = back[OWN]
    for slot in HELD:
        back_copy(slot).wait_recv()
        best = jnp.maximum(best, got[slot])

    amount = jnp.sum(jnp.where(member, best, 0.0), axis=1, keepdims=True)
    partial = numbers + jnp.sum(jnp.where(here & (sublane < CL_GRP), amount, 0.0), axis=0, keepdims=True)

    def exchange(buffer, value, me, partners, send, recv):
        buffer[me] = value
        copies = []
        for i, device in enumerate(partners):
            copies.append(pltpu.make_async_remote_copy(
                src_ref=buffer.at[me], dst_ref=buffer.at[me], send_sem=send.at[i], recv_sem=recv.at[i],
                device_id=device, device_id_type=MESH))
            copies[-1].start()
        return copies

    def total_of(buffer, copies):
        for c in copies:
            c.wait_recv()
        return functools.reduce(jnp.add, [buffer[i] for i in range(len(copies) + 1)])

    first = exchange(sums, partial, x * 4 + y, plane_devices, sum_send, sum_recv)
    best_ref[...] = best.reshape(rows)
    for slot in HELD:
        back_copy(slot).wait_send()
    part = total_of(sums, first)
    second = exchange(total, part, z * 4 + grp, column_devices, tot_send, tot_recv)
    for c in first:
        c.wait_send()
    whole = total_of(total, second)
    mean = whole / jnp.concatenate([whole[:, 64:], whole[:, :64]], axis=1)
    mean_ref[...] = mean.reshape(128)[:mean_ref.shape[0]]
    for c in second:
        c.wait_send()


def per_device(embeddings, cluster_ids):
    rows, width = embeddings.shape
    pieces = rows // PIECE
    dma = pltpu.SemaphoreType.DMA
    hbm = pl.BlockSpec(memory_space=pltpu.HBM)
    vmem = pl.BlockSpec(memory_space=pltpu.VMEM)
    return pl.pallas_call(
        kernel,
        out_shape=(jax.ShapeDtypeStruct((rows,), jnp.float32),
                   jax.ShapeDtypeStruct((CL_GRP * lax.axis_size("grp"),), jnp.float32)),
        in_specs=[hbm, hbm],
        out_specs=(vmem, vmem),
        scratch_shapes=[
            pltpu.VMEM((rows, width), jnp.bfloat16),
            pltpu.VMEM((rows,), jnp.int32),
            pltpu.VMEM((8, rows, width), jnp.bfloat16),
            pltpu.VMEM((7, rows, 128), jnp.float32),
            pltpu.VMEM((7, 8, rows), jnp.float32),
            pltpu.VMEM((7, rows, 128), jnp.float32),
            pltpu.VMEM((7, 8, rows), jnp.float32),
            pltpu.VMEM((8, 8, 128), jnp.float32),
            pltpu.VMEM((7, 1, rows), jnp.float32),
            pltpu.VMEM((7, 1, rows), jnp.float32),
            pltpu.VMEM((16, 1, 128), jnp.float32),
            pltpu.VMEM((8, 1, 128), jnp.float32),
            dma((pieces + 1,)),
            dma((7, pieces)), dma((7, pieces)),
            dma((7,)), dma((7,)),
            dma((6,)), dma((6,)),
            dma((15,)), dma((15,)),
            dma((7,)), dma((7,)),
            pltpu.SemaphoreType.REGULAR,
        ],
        compiler_params=pltpu.CompilerParams(collective_id=0, has_side_effects=True, vmem_limit_bytes=863 * 2**16 - 2**13),
    )(embeddings, cluster_ids)


def solution(mesh):
    placed = (P(("grp", "blk"), None), P(("grp", "blk")))
    return jax.shard_map(
        per_device, mesh=mesh, in_specs=placed, out_specs=(P(("grp", "blk")), P()), check_vma=False
    )
```

```python
import functools

import jax
import jax.numpy as jnp
from jax import lax
from jax.experimental import pallas as pl
from jax.experimental.pallas import tpu as pltpu
from jax.sharding import PartitionSpec as P

MESH = pl.DeviceIdType.MESH
CL_GRP = 3
FLOOR = -4.0
PIECE = 128
TILE = 256

OWN, B, C, F, G, A, E, RELAY = range(8)
HELD = {B: (1, 0, 0), C: (1, 1, 0), F: (0, 3, 1), G: (3, 0, 1), A: (3, 0, 0), E: (1, 2, 0)}
LINKS = {
    A: (OWN, (1, 0, 0)),
    B: (OWN, (3, 0, 0)),
    C: (B, (0, 3, 0)),
    E: (C, (0, 3, 0)),
    RELAY: (OWN, (0, 0, 1)),
    F: (RELAY, (0, 1, 0)),
    G: (RELAY, (1, 0, 0)),
}
WHOLE = ((B, OWN), (C, OWN), (C, B), (A, C), (F, OWN), (F, B), (F, C), (G, OWN), (G, B), (G, C), (G, F), (E, OWN))
HALVED = ((A, B), (A, F), (A, G), (E, B), (E, F), (E, G), (E, A))
PASS, SEND, TILE_OF, CUT = range(4)
ORDER = (
    (PASS, RELAY, 0),
    (TILE_OF, B, 0),
    (PASS, B, 0),
    (TILE_OF, B, 1),
    (PASS, B, 1),
    (PASS, B, 2),
    (PASS, RELAY, 1),
    (PASS, RELAY, 2),
    (PASS, B, 3),
    (PASS, C, 0),
    (PASS, C, 1),
    (PASS, B, 4),
    (TILE_OF, A, 0),
    (PASS, RELAY, 3),
    (TILE_OF, G, 0),
    (TILE_OF, F, 0),
    (PASS, B, 5),
    (PASS, C, 2),
    (PASS, RELAY, 4),
    (TILE_OF, C, 1),
    (TILE_OF, A, 1),
    (TILE_OF, B, 2),
    (TILE_OF, C, 0),
    (PASS, RELAY, 5),
    (SEND, A, 4),
    (SEND, A, 5),
    (PASS, C, 3),
    (TILE_OF, F, 1),
    (TILE_OF, E, 0),
    (PASS, C, 4),
    (PASS, C, 5),
    (TILE_OF, G, 1),
    (TILE_OF, C, 2),
    (CUT, OWN, 0),
    (TILE_OF, E, 1),
    (CUT, OWN, 0),
    (TILE_OF, G, 2),
    (TILE_OF, F, 2),
    (CUT, OWN, 0),
    (TILE_OF, E, 2),
    (TILE_OF, A, 2),
)


def kernel(x_hbm, ids_hbm, best_ref, mean_ref, x_ref, ids_ref, held, row_max, col_max, row_ids, col_ids, counts, back, got,
           sums, total, x_sem, send_sem, recv_sem, ids_send, ids_recv, back_send, back_recv, sum_send, sum_recv, tot_send,
           tot_recv, arrived):
    rows, width = x_ref.shape
    pieces, tiles = rows // PIECE, rows // TILE
    grp, blk = lax.axis_index("grp"), lax.axis_index("blk")
    x, y, z = blk // 8, (blk // 2) % 4, blk % 2
    swap = (z + grp) % 2

    def load(q):
        window = pl.ds(q * PIECE, PIECE)
        return pltpu.make_async_copy(x_hbm.at[window], x_ref.at[window], x_sem.at[q])

    load_ids = pltpu.make_async_copy(ids_hbm, ids_ref, x_sem.at[pieces])
    for q in range(pieces):
        load(q).start()
    load_ids.start()

    def place(nx, ny, nz):
        return (lax.rem(nx + 8, 4) * 4 + lax.rem(ny + 8, 4)) * 2 + lax.rem(nz, 2)

    def times(step):
        dx, dy, dz = step
        return (grp, place(x + dx * (1 - swap) + dy * swap, y + dy * (1 - swap) + dx * swap, z + dz))

    def in_plane(dx, dy):
        return (grp, place(x + dx, y + dy, z))

    def over(dz, dl, dc):
        return (lax.rem(grp // 2 + dl, 2) * 2 + lax.rem(grp + dc, 2), place(x, y, z + dz))

    plane = [(dx, dy) for dx in range(4) for dy in range(4) if dx or dy]
    plane.sort(key=lambda p: -sum(min(d, 4 - d) for d in p))
    same_core = [(1, 0, 0), (0, 1, 0), (1, 1, 0)]
    other_core = [(1, 0, 1), (0, 1, 1), (1, 1, 1), (0, 0, 1)]

    next_device = {slot: times(step) for slot, (_, step) in LINKS.items()}
    owner = {slot: times(step) for slot, step in HELD.items()}
    plane_devices = [in_plane(*p) for p in plane]
    column_devices = [over(*a) for a in same_core + other_core]

    barrier = pltpu.get_barrier_semaphore()
    greeted = [over(*a) for a in same_core] + [in_plane(*p) for p in ((0, 1), (0, 3), (1, 0), (3, 0))] + [over(0, 0, 1)]
    for device in greeted:
        pl.semaphore_signal(barrier, inc=1, device_id=device, device_id_type=MESH)

    def copy(slot, q):
        source = LINKS[slot][0]
        window = pl.ds(q * PIECE, PIECE)
        return pltpu.make_async_remote_copy(
            src_ref=held.at[source, window], dst_ref=held.at[slot, window], send_sem=send_sem.at[slot - 1, q],
            recv_sem=recv_sem.at[slot - 1, q], device_id=next_device[slot], device_id_type=MESH)

    def ids_copy(slot):
        source = LINKS[slot][0]
        return pltpu.make_async_remote_copy(
            src_ref=counts.at[source], dst_ref=counts.at[slot], send_sem=ids_send.at[slot - 1],
            recv_sem=ids_recv.at[slot - 1], device_id=next_device[slot], device_id_type=MESH)

    def back_copy(slot):
        return pltpu.make_async_remote_copy(
            src_ref=back.at[slot], dst_ref=got.at[slot], send_sem=back_send.at[slot - 1],
            recv_sem=back_recv.at[slot - 1], device_id=owner[slot], device_id_type=MESH)

    def normalise(q):
        load(q).wait()
        window = pl.ds(q * PIECE, PIECE)
        wide = x_ref[window, :].astype(jnp.float32)
        norms = jnp.sum(wide * wide, axis=1, keepdims=True)
        held[OWN, window, :] = (wide * lax.rsqrt(norms + 1e-06)).astype(jnp.bfloat16)

    def fill_ids(slot):
        low, high = counts[slot, 0:1, :], counts[slot, 1:2, :]
        at = lax.broadcasted_iota(jnp.int32, (rows, 128), 0).astype(jnp.float32)
        row_ids[slot] = (at >= low).astype(jnp.float32) + (at >= high).astype(jnp.float32)
        for j in range(rows // 128):
            at = (lax.broadcasted_iota(jnp.int32, (8, 128), 1) + 128 * j).astype(jnp.float32)
            col_ids[slot, :, pl.ds(128 * j, 128)] = (at >= low).astype(jnp.float32) + (at >= high).astype(jnp.float32)

    def product(j, first, n, s, q, diagonal=False):
        window = pl.ds(q * TILE, TILE)
        scores = lax.dot_general(held[j, pl.ds(first, n), :], held[s, window, :], (((1,), (1,)), ((), ())),
                                 preferred_element_type=jnp.float32)
        ids = row_ids[j, pl.ds(first, n), :]
        same = jnp.concatenate([ids] * (TILE // 128), axis=1) == col_ids[s, 0:1, window]
        if diagonal:
            same = same & (lax.broadcasted_iota(jnp.int32, (n, TILE), 0) != lax.broadcasted_iota(jnp.int32, (n, TILE), 1))
        masked = jnp.where(same, scores, jnp.float32(FLOOR))
        across_tile = functools.reduce(jnp.maximum, [masked[:, 128 * t:128 * t + 128] for t in range(TILE // 128)])
        row_max[j, pl.ds(first, n), :] = jnp.maximum(row_max[j, pl.ds(first, n), :], across_tile)
        if not diagonal:
            down = jnp.max(masked.reshape(n // 8, 8, TILE), axis=0)
            col_max[s, :, window] = jnp.maximum(col_max[s, :, window], down)

    waited, ready, tiles_in = set(), set(), set()

    def wait(slot, q):
        if (slot, q) not in waited:
            waited.add((slot, q))
            copy(slot, q).wait_recv()

    def wait_ids(slot):
        if slot not in ready:
            ready.add(slot)
            ids_copy(slot).wait_recv()
            if slot != RELAY:
                fill_ids(slot)

    def wait_tile(s, q):
        for p in range(q * TILE // PIECE, (q + 1) * TILE // PIECE):
            wait(s, p)
        wait_ids(s)

    def wanted(s, q, j, r):
        if (s, j) in WHOLE or (j, s) in WHOLE:
            return True
        return ((s, j) in HALVED and r >= q) or ((j, s) in HALVED and q >= r)

    def multiply(s, q):
        tiles_in.add((s, q))
        if s == OWN:
            product(OWN, q * TILE, TILE, OWN, q, diagonal=True)
            if q + 1 < tiles:
                product(OWN, (q + 1) * TILE, rows - (q + 1) * TILE, OWN, q)
            return
        wait_tile(s, q)
        for j in (OWN, *HELD):
            if j == s:
                continue
            r = 0
            while r < tiles:
                end = r
                while end < tiles and (j, end) in tiles_in and wanted(s, q, j, end):
                    end += 1
                if end > r:
                    product(j, r * TILE, (end - r) * TILE, s, q)
                r = end + 1

    def pass_on(slot, q):
        wait(slot, q)
        onward = [to for to, (source, _) in LINKS.items() if source == slot]
        for to in onward:
            copy(to, q).start()
        if q == 0:
            wait_ids(slot)
            for to in onward:
                ids_copy(to).start()

    load_ids.wait()
    ids = ids_ref[...].reshape(1, rows)
    base = grp * CL_GRP
    low = jnp.sum((ids <= base).astype(jnp.float32), axis=1, keepdims=True)
    high = jnp.sum((ids <= base + 1).astype(jnp.float32), axis=1, keepdims=True)
    counts[OWN] = jnp.where(lax.broadcasted_iota(jnp.int32, (8, 128), 0) == 0, low, high)

    for q in range(pieces):
        normalise(q)
    fill_ids(OWN)
    row_max[...] = jnp.full_like(row_max, FLOOR)
    col_max[...] = jnp.full_like(col_max, FLOOR)
    for q in range(tiles):
        multiply(OWN, q)

    pl.semaphore_wait(barrier, len(greeted))
    early = [q for q in range(pieces) if (SEND, A, q) not in ORDER]
    for q in range(pieces):
        for slot in (B, RELAY, A):
            if slot != A or q in early:
                copy(slot, q).start()
            if q == 0:
                ids_copy(slot).start()
    for a in same_core:
        pl.semaphore_signal(arrived, inc=1, device_id=over(*a), device_id_type=MESH)
    relative = col_ids[OWN, 0:1, :]
    sublane = lax.broadcasted_iota(jnp.int32, (8, 1), 0)
    lane = lax.broadcasted_iota(jnp.int32, (8, 128), 1)
    member = relative == sublane.astype(jnp.float32)
    number = jnp.sum(member.astype(jnp.float32), axis=1, keepdims=True)
    here = lane == base + sublane
    numbers = jnp.sum(jnp.where((lane == base + sublane + 64) & (sublane < CL_GRP), number, 0.0), axis=0, keepdims=True)

    for i, (action, slot, q) in enumerate(ORDER):
        if action == PASS:
            pass_on(slot, q)
        elif action == SEND:
            copy(slot, q).start()
        elif action == TILE_OF:
            for group_action, s, t in ORDER[i:]:
                if group_action != TILE_OF:
                    break
                wait_tile(s, t)
            multiply(slot, q)

    def finish(slot):
        for j in range(rows // 128):
            window = pl.ds(128 * j, 128)
            across_rows = jnp.max(row_max[slot, window, :].T, axis=0, keepdims=True)
            back[slot, :, window] = jnp.maximum(across_rows, jnp.max(col_max[slot, :, window], axis=0, keepdims=True))

    for slot in (E, F, G, C, A, B):
        finish(slot)
        back_copy(slot).start()
    finish(OWN)
    for slot in LINKS:
        for q in range(pieces):
            copy(slot, q).wait_send()
        ids_copy(slot).wait_send()
    pl.semaphore_wait(arrived, len(same_core))
    best = back[OWN]
    for slot in HELD:
        back_copy(slot).wait_recv()
        best = jnp.maximum(best, got[slot])

    amount = jnp.sum(jnp.where(member, best, 0.0), axis=1, keepdims=True)
    partial = numbers + jnp.sum(jnp.where(here & (sublane < CL_GRP), amount, 0.0), axis=0, keepdims=True)

    def exchange(buffer, value, me, partners, send, recv):
        buffer[me] = value
        copies = []
        for i, device in enumerate(partners):
            copies.append(pltpu.make_async_remote_copy(
                src_ref=buffer.at[me], dst_ref=buffer.at[me], send_sem=send.at[i], recv_sem=recv.at[i],
                device_id=device, device_id_type=MESH))
            copies[-1].start()
        return copies

    def total_of(buffer, copies):
        for c in copies:
            c.wait_recv()
        return functools.reduce(jnp.add, [buffer[i] for i in range(len(copies) + 1)])

    first = exchange(sums, partial, x * 4 + y, plane_devices, sum_send, sum_recv)
    best_ref[...] = best.reshape(rows)
    for slot in HELD:
        back_copy(slot).wait_send()
    part = total_of(sums, first)
    second = exchange(total, part, z * 4 + grp, column_devices, tot_send, tot_recv)
    for c in first:
        c.wait_send()
    whole = total_of(total, second)
    mean = whole / jnp.concatenate([whole[:, 64:], whole[:, :64]], axis=1)
    mean_ref[...] = mean.reshape(128)[:mean_ref.shape[0]]
    for c in second:
        c.wait_send()


def per_device(embeddings, cluster_ids):
    rows, width = embeddings.shape
    pieces = rows // PIECE
    dma = pltpu.SemaphoreType.DMA
    hbm = pl.BlockSpec(memory_space=pltpu.HBM)
    vmem = pl.BlockSpec(memory_space=pltpu.VMEM)
    return pl.pallas_call(
        kernel,
        out_shape=(jax.ShapeDtypeStruct((rows,), jnp.float32),
                   jax.ShapeDtypeStruct((CL_GRP * lax.axis_size("grp"),), jnp.float32)),
        in_specs=[hbm, hbm],
        out_specs=(vmem, vmem),
        scratch_shapes=[
            pltpu.VMEM((rows, width), jnp.bfloat16),
            pltpu.VMEM((rows,), jnp.int32),
            pltpu.VMEM((8, rows, width), jnp.bfloat16),
            pltpu.VMEM((7, rows, 128), jnp.float32),
            pltpu.VMEM((7, 8, rows), jnp.float32),
            pltpu.VMEM((7, rows, 128), jnp.float32),
            pltpu.VMEM((7, 8, rows), jnp.float32),
            pltpu.VMEM((8, 8, 128), jnp.float32),
            pltpu.VMEM((7, 1, rows), jnp.float32),
            pltpu.VMEM((7, 1, rows), jnp.float32),
            pltpu.VMEM((16, 1, 128), jnp.float32),
            pltpu.VMEM((8, 1, 128), jnp.float32),
            dma((pieces + 1,)),
            dma((7, pieces)), dma((7, pieces)),
            dma((7,)), dma((7,)),
            dma((6,)), dma((6,)),
            dma((15,)), dma((15,)),
            dma((7,)), dma((7,)),
            pltpu.SemaphoreType.REGULAR,
        ],
        compiler_params=pltpu.CompilerParams(collective_id=0, has_side_effects=True, vmem_limit_bytes=863 * 2**16 - 2**13),
    )(embeddings, cluster_ids)


def solution(mesh):
    placed = (P(("grp", "blk"), None), P(("grp", "blk")))
    return jax.shard_map(
        per_device, mesh=mesh, in_specs=placed, out_specs=(P(("grp", "blk")), P()), check_vma=False
    )
```
